256 devices in a mesh: user: 16 (over y, x), track: 16 (over z, core).
Axes of the slice: x: 4, y: 4, z: 8, core: 2. Of those that a mesh axis runs over, the one named last changes fastest.
Arguments:
- user_emb: float32 [32768, 128], P(('user', 'track')), may hold values from -6 to 6
- user_cot: float32 [32768, 128], P(('user', 'track')), may hold values from -6 to 6
- track_emb: float32 [32768, 128], P('track'), may hold values from -6 to 6
- track_cot: float32 [32768, 128], P('track'), may hold values from -6 to 6
- user_degree: int32 [32768], P(('user', 'track')), may hold values from 32768 to 131071
- track_degree: int32 [32768], P('track'), may hold values from 32768 to 131071
- tile_vals: float32 [16, 16, 128, 128, 128], P('user', 'track'), may hold values from 0 to 512
- tile_rows: int32 [16, 16, 128], P('user', 'track'), may hold values from 0 to 15
- tile_cols: int32 [16, 16, 128], P('user', 'track'), may hold values from 0 to 15
- tile_count: int32 [16, 16], P('user', 'track'), may hold values from 12 to 128, as said below
Outputs:
- user_out: float32 [32768, 128], P(('user', 'track'))
- user_grad: float32 [32768, 128], P(('user', 'track'))
- track_out: float32 [16, 16, 128, 128], P('user', 'track')
- track_grad: float32 [16, 16, 128, 128], P('user', 'track')
The draws below stay inside these ranges and needn't reach their ends.
Inputs may be any that keep to these rules, and one draw needn't show every extreme that they name: Only the first tile_count[a, b] slots of grid cell (a, b) hold tiles; some cell is full in every draw. Live slots may repeat a tile position, and then their tiles add.
All inputs are finite; a program needn't handle non-finite values.
Results may differ from the reference program's by a relative error of at most 0.0003.
Values sent between devices are 32-bit elements; how exact they have to be, the bound alone decides.
No kernel may reach another device: no remote copies, remote signals or barrier semaphores. Data moves between devices by JAX's collectives and lax.ppermute only.
A program may use at most 128 MiB of HBM per device.

```python
import jax
import jax.numpy as jnp
from jax import lax

EMB = 128
TILE = 128
USER_TILES = 16
TRACK_TILES = 16
SLOTS = 128
USERS = 32768
TRACKS = 32768
N_USER = 16
N_TRACK = 16


def draw_tile_count(key, part):
    key = jax.random.fold_in(key, 7)
    key_halve, key_jitter, key_chosen = jax.random.split(key, 3)
    device_total = N_USER * N_TRACK
    halvings = jax.random.randint(key_halve, (device_total,), 0, 4)
    full_count = jnp.right_shift(jnp.full((device_total,), SLOTS, jnp.int32), halvings)
    jitter = jax.random.randint(key_jitter, (device_total,), 0, 1 << 20) % (full_count // 4 + 1)
    counts = full_count - jitter
    chosen = jax.random.randint(key_chosen, (), 0, device_total)
    counts = jnp.where(jnp.arange(device_total) == chosen, SLOTS, counts)
    return counts.reshape(N_USER, N_TRACK).astype(jnp.int32)


def touch_ends(array, rng, least, high):
    shape = array.shape
    place = [jax.random.randint(jax.random.fold_in(rng, axis), (), 0, shape[axis]) for axis in range(len(shape))]
    array = array.at[tuple(place)].set(least)
    longest = shape.index(max(shape))
    place[longest] = (place[longest] + 1) % shape[longest]
    return array.at[tuple(place)].set(high)


def block_scale(own_key, extent, cuts, low, largest):
    level = 1.0
    for position, shards_of in cuts:
        heights = jax.random.uniform(jax.random.fold_in(jax.random.fold_in(own_key, 6), position), (shards_of,), jnp.float32, low / len(cuts), largest / len(cuts))
        level = level * jnp.repeat(jnp.exp(heights), extent[position] // shards_of).reshape((-1,) + (1,) * (len(extent) - 1 - position))
    return level


def bell_draw(own_key, extent, deviation, reach, cuts=(), held_as=jnp.bfloat16):
    gain = block_scale(own_key, extent, cuts, -0.22, 0.18) if cuts else 1.0
    entries = jax.random.normal(own_key, extent, jnp.float32) * deviation * gain
    return jnp.minimum(jnp.maximum(entries, -reach), reach).astype(held_as)


def setup_inputs(seed: int = 0) -> dict:
    splits = jax.random.split(jax.random.key(seed), 11)
    user_emb = bell_draw(splits[0], (USERS, EMB), 1.0, 6.0, ((0, 256),), jnp.float32)
    user_cot = bell_draw(splits[1], (USERS, EMB), 1.0, 6.0, ((0, 256),), jnp.float32)
    track_emb = bell_draw(splits[2], (TRACKS, EMB), 1.0, 6.0, ((0, 16),), jnp.float32)
    track_cot = bell_draw(splits[3], (TRACKS, EMB), 1.0, 6.0, ((0, 16),), jnp.float32)
    user_degree = touch_ends(jax.random.randint(splits[4], (USERS,), 2 * N_TRACK * SLOTS * TILE // USER_TILES, 8 * N_TRACK * SLOTS * TILE // USER_TILES), jax.random.fold_in(splits[4], 1), 2 * N_TRACK * SLOTS * TILE // USER_TILES, (8 * N_TRACK * SLOTS * TILE // USER_TILES) - 1).astype(jnp.int32)
    track_degree = touch_ends(jax.random.randint(splits[5], (TRACKS,), 2 * N_USER * SLOTS * TILE // TRACK_TILES, 8 * N_USER * SLOTS * TILE // TRACK_TILES), jax.random.fold_in(splits[5], 1), 2 * N_USER * SLOTS * TILE // TRACK_TILES, (8 * N_USER * SLOTS * TILE // TRACK_TILES) - 1).astype(jnp.int32)
    tile_vals = jnp.clip(512.0 * jax.random.uniform(splits[6], (N_USER, N_TRACK, SLOTS, TILE, TILE), jnp.float32) ** block_scale(splits[6], (N_USER, N_TRACK, SLOTS, TILE, TILE), ((0, 16), (1, 16)), -0.2, 0.2), 0.0, 512.0)
    tile_rows = touch_ends(jax.random.randint(splits[7], (N_USER, N_TRACK, SLOTS), 0, USER_TILES), jax.random.fold_in(splits[7], 1), 0, USER_TILES - 1).astype(jnp.int32)
    tile_cols = touch_ends(jax.random.randint(splits[8], (N_USER, N_TRACK, SLOTS), 0, TRACK_TILES), jax.random.fold_in(splits[8], 1), 0, TRACK_TILES - 1).astype(jnp.int32)
    tile_count = draw_tile_count(jax.random.fold_in(splits[10], 71), 0)
    return dict(user_emb=user_emb, user_cot=user_cot, track_emb=track_emb, track_cot=track_cot, user_degree=user_degree, track_degree=track_degree, tile_vals=tile_vals, tile_rows=tile_rows, tile_cols=tile_cols, tile_count=tile_count)


def reference(user_emb, user_cot, track_emb, track_cot, user_degree, track_degree, tile_vals, tile_rows, tile_cols, tile_count):
    highest = lax.Precision.HIGHEST
    user_scale = 1.0 / jnp.sqrt(user_degree.astype(jnp.float32))
    track_scale = 1.0 / jnp.sqrt(track_degree.astype(jnp.float32))
    user_side = (jnp.concatenate([user_emb, user_cot], axis=1) * user_scale[:, None]).reshape(USERS // TILE, TILE, 2 * EMB)
    track_side = (jnp.concatenate([track_emb, track_cot], axis=1) * track_scale[:, None]).reshape(TRACKS // TILE, TILE, 2 * EMB)
    slot_ids = jnp.arange(SLOTS, dtype=jnp.int32)

    def one_device(totals, device):
        user_acc, track_acc = totals
        user_block = device // N_TRACK
        track_block = device % N_TRACK
        live_mask = (slot_ids < tile_count[user_block, track_block]).astype(jnp.float32)
        values = tile_vals[user_block, track_block] * live_mask[:, None, None]
        row_ids = (user_block * USER_TILES + tile_rows[user_block, track_block]).astype(jnp.int32)
        col_ids = (tile_cols[user_block, track_block] * N_TRACK + track_block).astype(jnp.int32)
        to_users = jnp.einsum('kij,kje->kie', values, track_side[col_ids], precision=highest)
        to_tracks = jnp.einsum('kij,kie->kje', values, user_side[row_ids], precision=highest)
        return ((user_acc.at[row_ids].add(to_users), track_acc.at[col_ids].add(to_tracks)), None)
    zero_sums = (jnp.zeros(user_side.shape, jnp.float32), jnp.zeros(track_side.shape, jnp.float32))
    (user_acc, track_acc), ignored = lax.scan(one_device, zero_sums, jnp.arange(N_USER * N_TRACK, dtype=jnp.int32))
    user_res = user_acc.reshape(USERS, 2 * EMB) * user_scale[:, None]
    track_res = (track_acc.reshape(TRACKS, 2 * EMB) * track_scale[:, None]).reshape(TRACK_TILES, N_TRACK, TILE, 2 * EMB)
    return (user_res[:, :EMB], user_res[:, EMB:], track_res[..., :EMB], track_res[..., EMB:])
```

```python
import jax
import jax.numpy as jnp
from jax import lax
from jax.experimental import pallas as pl
from jax.experimental.pallas import tpu as pltpu
from jax.sharding import PartitionSpec as P

TILE = 128
TILES = 16
EMB = 128
SLOTS = 128
SLOT_STEP = 16
BLOCK = 256
MIB = 1 << 20
F32 = jnp.float32
BF16 = jnp.bfloat16


def rows_of(i, size):
    return pl.ds(pl.multiple_of(i * size, size), size)


def split_hi_lo(x):
    hi = x.astype(BF16)
    return hi, (x - hi.astype(F32)).astype(BF16)


def build_kernel(row_ref, col_ref, count_ref, vals_ref, hi_ref, lo_ref, slots, dense, hi, lo, sems):
    loads = SLOTS // SLOT_STEP
    copies = []
    for i in range(loads):
        part = pl.ds(i * SLOT_STEP, SLOT_STEP)
        copies.append(pltpu.make_async_copy(vals_ref.at[part], slots.at[part], sems.at[i]))
        copies[-1].start()

    def clear(i, carry):
        dense[i] = jnp.zeros((TILE, TILE), F32)
        return carry

    lax.fori_loop(0, TILES * TILES, clear, 0)

    def add(s, carry):
        dense[row_ref[s] * TILES + col_ref[s]] += slots[s]
        return carry

    for i in range(loads):
        copies[i].wait()
        live = jnp.clip(count_ref[0], i * SLOT_STEP, (i + 1) * SLOT_STEP)
        lax.fori_loop(i * SLOT_STEP, live, add, 0)

    copies = []
    for b in range(SIZE // BLOCK):

        def pack(r, carry):
            rows = rows_of(r, TILE)
            for c in range(TILES):
                high, low = split_hi_lo(dense[r * TILES + c])
                hi[rows, c * TILE : (c + 1) * TILE] = high
                lo[rows, c * TILE : (c + 1) * TILE] = low
            return carry

        lax.fori_loop(2 * b, 2 * b + 2, pack, 0)
        rows = pl.ds(b * BLOCK, BLOCK)
        copies.append(pltpu.make_async_copy(hi.at[rows], hi_ref.at[rows], sems.at[2 * b]))
        copies.append(pltpu.make_async_copy(lo.at[rows], lo_ref.at[rows], sems.at[2 * b + 1]))
        copies[-2].start()
        copies[-1].start()
    for copy in copies:
        copy.wait()


VMEM = pl.BlockSpec(memory_space=pltpu.VMEM)
SMEM = pl.BlockSpec(memory_space=pltpu.SMEM)
HBM = pl.BlockSpec(memory_space=pltpu.HBM)
SIZE = TILES * TILE
BLOCKS = SIZE // BLOCK
DEPTH = 3


def build(vals, rows, cols, count):
    return pl.pallas_call(
        build_kernel,
        in_specs=[SMEM, SMEM, SMEM, HBM],
        out_specs=[HBM, HBM],
        out_shape=[jax.ShapeDtypeStruct((SIZE, SIZE), BF16)] * 2,
        scratch_shapes=[
            pltpu.VMEM((SLOTS, TILE, TILE), F32),
            pltpu.VMEM((TILES * TILES, TILE, TILE), F32),
            pltpu.VMEM((SIZE, SIZE), BF16),
            pltpu.VMEM((SIZE, SIZE), BF16),
            pltpu.SemaphoreType.DMA((2 * BLOCKS,)),
        ],
        compiler_params=pltpu.CompilerParams(vmem_limit_bytes=48 * MIB),
        cost_estimate=pl.CostEstimate(flops=0, bytes_accessed=24 * MIB, transcendentals=0),
    )(rows, cols, count, vals)


def stream(hi_ref, lo_ref, hi, lo, sems, part):
    def copies(b):
        at = part(b)
        return [
            pltpu.make_async_copy(hi_ref.at[at], hi.at[at], sems.at[0, b]),
            pltpu.make_async_copy(lo_ref.at[at], lo.at[at], sems.at[1, b]),
        ]

    def begin(b):
        for copy in copies(b):
            copy.start()

    def finish(b):
        for copy in copies(b):
            copy.wait()

        @pl.when(b + DEPTH < BLOCKS)
        def _():
            begin(b + DEPTH)

    for b in range(DEPTH):
        begin(b)
    return finish


def track_kernel(place_ref, *refs):
    blocks, (theirs_ref, hi_ref, lo_ref, out_ref, phi, plo, hi, lo, sems) = refs[:8], refs[8:]
    core = place_ref[1]
    finish = stream(
        hi_ref, lo_ref, hi, lo, sems, lambda b: (slice(None), rows_of(b, BLOCK))
    )

    def put(tile, x):
        high, low = split_hi_lo(x.T)
        at = rows_of(tile, TILE)
        phi[:, at] = high
        plo[:, at] = low

    for d in range(8):
        z = lax.rem(place_ref[0] + d, 8)
        put(2 * z + core, blocks[d][...])
        put(2 * z + 1 - core, theirs_ref[d])

    def one(b, carry):
        at = rows_of(b, BLOCK)
        finish(b)
        out = jnp.dot(phi[...], hi[:, at], preferred_element_type=F32)
        out += jnp.dot(plo[...], hi[:, at], preferred_element_type=F32)
        out += jnp.dot(phi[...], lo[:, at], preferred_element_type=F32)
        out_ref[at, :] = out.T
        return carry

    lax.fori_loop(0, BLOCKS, one, 0)


STREAM = [pltpu.VMEM((SIZE, SIZE), BF16)] * 2 + [pltpu.SemaphoreType.DMA((2, BLOCKS))]


def cost(flops):
    return pl.CostEstimate(flops=flops, bytes_accessed=1024, transcendentals=0)


def track_sums(place, blocks, theirs, hi, lo):
    return pl.pallas_call(
        track_kernel,
        in_specs=[SMEM] + [VMEM] * 9 + [HBM] * 2,
        out_specs=VMEM,
        scratch_shapes=[pltpu.VMEM((2 * EMB, SIZE), BF16)] * 2 + STREAM,
        out_shape=jax.ShapeDtypeStruct((SIZE, 2 * EMB), F32),
        compiler_params=pltpu.CompilerParams(vmem_limit_bytes=56 * MIB),
        cost_estimate=cost(0),
    )(place, *blocks, theirs, hi, lo)


def user_kernel(place_ref, *refs):
    embs, cots = refs[:4], refs[4:8]
    hi_ref, lo_ref, keep_ref, send_ref, phi, plo, sums, hi, lo, sems = refs[8:]
    share = TILE // 4

    def block(b):
        return rows_of(lax.rem(place_ref[0] + b, 8), BLOCK)

    finish = stream(hi_ref, lo_ref, hi, lo, sems, lambda b: (block(b), slice(None)))

    def put(pieces, start, lanes):
        for d in range(4):
            at = rows_of(lax.rem(start + d, 4), share)

            def tile(c, carry):
                high, low = split_hi_lo(pieces[d][c])
                phi[c, at, lanes] = high
                plo[c, at, lanes] = low
                return carry

            lax.fori_loop(0, TILES, tile, 0, unroll=4)

    put(embs, place_ref[3], slice(0, EMB))
    put(cots, place_ref[2], slice(EMB, 2 * EMB))
    core = place_ref[1]

    def one(b, carry):
        at = block(b)
        finish(b)
        panel_hi = phi[...].reshape(SIZE, 2 * EMB)
        out = jnp.dot(hi[at, :], panel_hi, preferred_element_type=F32)
        out += jnp.dot(lo[at, :], panel_hi, preferred_element_type=F32)
        panel_lo = plo[...].reshape(SIZE, 2 * EMB)
        out += jnp.dot(hi[at, :], panel_lo, preferred_element_type=F32)
        sums[...] = out
        keep_ref[b] = sums[rows_of(core, TILE), :]
        send_ref[b] = sums[rows_of(1 - core, TILE), :]
        return carry

    lax.fori_loop(0, BLOCKS, one, 0)


def user_sums(place, embs, cots, hi, lo):
    return pl.pallas_call(
        user_kernel,
        in_specs=[SMEM] + [VMEM] * 8 + [HBM] * 2,
        out_specs=[VMEM] * 2,
        scratch_shapes=[
            pltpu.VMEM((TILES, TILE, 2 * EMB), BF16),
            pltpu.VMEM((TILES, TILE, 2 * EMB), BF16),
            pltpu.VMEM((BLOCK, 2 * EMB), F32),
        ]
        + STREAM,
        out_shape=[jax.ShapeDtypeStruct((8, TILE, 2 * EMB), F32)] * 2,
        compiler_params=pltpu.CompilerParams(vmem_limit_bytes=56 * MIB),
        cost_estimate=cost(0),
    )(place, *embs, *cots, hi, lo)


def shift_z(x, by):
    pairs = [(2 * z + c, 2 * ((z + by) % 8) + c) for z in range(8) for c in range(2)]
    return lax.ppermute(x, "track", pairs)


def swap_core(x):
    return lax.ppermute(x, "track", [(t, t ^ 1) for t in range(16)])


def shift_x(x, by):
    pairs = [(4 * j + i, 4 * j + (i + by) % 4) for j in range(4) for i in range(4)]
    return lax.ppermute(x, "user", pairs)


def shift_y(x, by):
    pairs = [(4 * j + i, 4 * ((j + by) % 4) + i) for j in range(4) for i in range(4)]
    return lax.ppermute(x, "user", pairs)


def from_all(shift, x):
    far, right, left = shift(x, 2), shift(x, -1), shift(x, 1)
    return [x, right, far, left]


def body(
    user_emb,
    user_cot,
    track_emb,
    track_cot,
    user_degree,
    track_degree,
    tile_vals,
    tile_rows,
    tile_cols,
    tile_count,
):
    user = lax.axis_index("user").astype(jnp.int32)
    track = lax.axis_index("track").astype(jnp.int32)
    place = jnp.stack([track // 2, track % 2, user // 4, user % 4])
    user_scale = 1.0 / jnp.sqrt(user_degree.astype(F32))
    track_scale = 1.0 / jnp.sqrt(track_degree.astype(F32))

    share = TILE // 4
    scales = track_scale.reshape(TILES, TILE, 1)

    def part(x, which):
        x = x.reshape(TILES, TILE, EMB) * scales
        return lax.dynamic_slice_in_dim(x, which * share, share, 1)

    moving = jnp.concatenate(
        [part(track_emb, user % 4), part(track_cot, user // 4), scales.reshape(TILES, 1, TILE)],
        axis=1,
    )
    arrived = lax.all_to_all(moving, "track", split_axis=0, concat_axis=0, tiled=True)

    user_piece = jnp.concatenate([user_emb, user_cot], axis=1) * user_scale[:, None]
    hi, lo = build(
        tile_vals.reshape(SLOTS, TILE, TILE),
        tile_rows.reshape(SLOTS),
        tile_cols.reshape(SLOTS),
        tile_count.reshape(1),
    )
    blocks = [user_piece] + [None] * 7
    for d in range(1, 5):
        blocks[d] = shift_z(blocks[d - 1], -1)
        if d < 4:
            blocks[8 - d] = shift_z(blocks[(9 - d) % 8], 1)
        if d == 1:
            blocks[1], blocks[7], hi = lax.optimization_barrier((blocks[1], blocks[7], hi))
    arrived, hi = lax.optimization_barrier((arrived, hi))
    own_scale = lax.dynamic_slice_in_dim(arrived[:, 2 * share], user, 1, 0).reshape(TILE, 1)
    embs = from_all(shift_x, arrived[:, :share])
    cots = from_all(shift_y, arrived[:, share : 2 * share])

    mine, embs, cots = lax.optimization_barrier((jnp.stack(blocks), embs, cots))
    theirs = swap_core(mine)
    to_tracks = track_sums(place, blocks, theirs, hi, lo)
    to_tracks, embs, cots = lax.optimization_barrier((to_tracks, embs, cots))
    landed = lax.all_to_all(
        to_tracks.reshape(TILES, TILE, 2 * EMB), "user", split_axis=0, concat_axis=0, tiled=True
    )

    keep, send = user_sums(place, embs, cots, hi, lo)
    got = swap_core(send)
    up = shift_z(keep[4] + got[4], 1)
    down = shift_z(keep[5] + got[5], -1)
    for d in (3, 2, 1):
        up = up + (keep[d] + got[d])
        if d == 1:
            up, landed = lax.optimization_barrier((up, landed))
        up = shift_z(up, 1)
        if d > 1:
            down = shift_z(down + (keep[9 - d] + got[9 - d]), -1)
    user_total = (keep[0] + got[0] + up + down) * user_scale[:, None]
    track_total = (jnp.sum(landed, axis=0) * own_scale).reshape(1, 1, TILE, 2 * EMB)
    return (
        user_total[:, :EMB],
        user_total[:, EMB:],
        track_total[..., :EMB],
        track_total[..., EMB:],
    )


def solution(mesh):
    placed = (
        P(("user", "track"), None),
        P(("user", "track"), None),
        P("track", None),
        P("track", None),
        P(("user", "track")),
        P("track"),
        P("user", "track", None, None, None),
        P("user", "track", None),
        P("user", "track", None),
        P("user", "track"),
    )
    return jax.shard_map(
        body,
        mesh=mesh,
        in_specs=placed,
        out_specs=(
            P(("user", "track"), None),
            P(("user", "track"), None),
            P("user", "track", None, None),
            P("user", "track", None, None),
        ),
        check_vma=False,
    )
```

```python
import functools

import jax
import jax.numpy as jnp
from jax import lax
from jax.experimental import pallas as pl
from jax.experimental.pallas import tpu as pltpu
from jax.sharding import PartitionSpec as P

TILE = 128
TILES = 16
EMB = 128
SLOTS = 128
SLOT_STEP = 16
HALF = TILES // 2
BLOCK = 256
MIB = 1 << 20
F32 = jnp.float32
BF16 = jnp.bfloat16


def rows_of(i, size):
    return pl.ds(pl.multiple_of(i * size, size), size)


def split_hi_lo(x):
    hi = x.astype(BF16)
    return hi, (x - hi.astype(F32)).astype(BF16)


def build_kernel(half, row_ref, col_ref, count_ref, vals_ref, *refs):
    out_ref, slots, dense, hi, lo, sems = refs[-6:]
    loads = SLOTS // SLOT_STEP
    copies = []
    for i in range(loads):
        part = pl.ds(i * SLOT_STEP, SLOT_STEP)
        copies.append(pltpu.make_async_copy(vals_ref.at[part], slots.at[part], sems.at[i]))
        copies[-1].start()

    def clear(i, carry):
        dense[i] = jnp.zeros((TILE, TILE), F32)
        return carry

    lax.fori_loop(0, HALF * TILES, clear, 0)

    def add(s, carry):
        row = row_ref[s] - half * HALF

        @pl.when((row >= 0) & (row < HALF))
        def _():
            dense[row * TILES + col_ref[s]] += slots[s]

        return carry

    for i in range(loads):
        copies[i].wait()
        live = jnp.clip(count_ref[0], i * SLOT_STEP, (i + 1) * SLOT_STEP)
        lax.fori_loop(i * SLOT_STEP, live, add, 0)

    copies = []
    for b in range(HALF // 2):

        def pack(r, carry):
            rows = rows_of(r, TILE)
            for c in range(TILES):
                high, low = split_hi_lo(dense[r * TILES + c])
                hi[rows, c * TILE : (c + 1) * TILE] = high
                lo[rows, c * TILE : (c + 1) * TILE] = low
            return carry

        lax.fori_loop(2 * b, 2 * b + 2, pack, 0)
        rows = pl.ds(b * BLOCK, BLOCK)
        there = pl.ds(half * HALF * TILE + b * BLOCK, BLOCK)
        copies.append(pltpu.make_async_copy(hi.at[rows], out_ref.at[0, there], sems.at[2 * b]))
        copies.append(pltpu.make_async_copy(lo.at[rows], out_ref.at[1, there], sems.at[2 * b + 1]))
        copies[-2].start()
        copies[-1].start()
    for copy in copies:
        copy.wait()


VMEM = pl.BlockSpec(memory_space=pltpu.VMEM)
SMEM = pl.BlockSpec(memory_space=pltpu.SMEM)
HBM = pl.BlockSpec(memory_space=pltpu.HBM)
SIZE = TILES * TILE
BLOCKS = SIZE // BLOCK
DEPTH = 3
STREAM = [pltpu.SemaphoreType.DMA((DEPTH, 2))]


def cost(nbytes):
    return pl.CostEstimate(flops=0, bytes_accessed=nbytes, transcendentals=0)


def build(half, vals, rows, cols, count, *others):
    return pl.pallas_call(
        functools.partial(build_kernel, half),
        in_specs=[SMEM, SMEM, SMEM, HBM] + [HBM] * len(others),
        out_specs=HBM,
        out_shape=jax.ShapeDtypeStruct((2, SIZE, SIZE), BF16),
        input_output_aliases={4: 0} if others else {},
        scratch_shapes=[
            pltpu.VMEM((SLOTS, TILE, TILE), F32),
            pltpu.VMEM((HALF * TILES, TILE, TILE), F32),
            pltpu.VMEM((HALF * TILE, SIZE), BF16),
            pltpu.VMEM((HALF * TILE, SIZE), BF16),
            pltpu.SemaphoreType.DMA((SLOTS // SLOT_STEP,)),
        ],
        compiler_params=pltpu.CompilerParams(vmem_limit_bytes=46 * MIB),
        cost_estimate=cost(12 * MIB * half),
    )(rows, cols, count, vals, *others)


def stream(adj_ref, slots, sems, part):
    def copies(b):
        at = part(b)
        slot = lax.rem(b, DEPTH)
        return [
            pltpu.make_async_copy(adj_ref.at[(k,) + at], slots.at[slot, k], sems.at[slot, k])
            for k in range(2)
        ]

    def begin(b):
        for copy in copies(b):
            copy.start()

    def finish(b):
        for copy in copies(b):
            copy.wait()
        slot = lax.rem(b, DEPTH)
        return slots[slot, 0], slots[slot, 1]

    def after(b):
        @pl.when(b + DEPTH < BLOCKS)
        def _():
            begin(b + DEPTH)

    for b in range(DEPTH):
        begin(b)
    return finish, after


def track_kernel(*refs):
    blocks, (theirs_ref, adj_ref, out_ref, phi, plo, slots, sems) = refs[:8], refs[8:]
    track = lax.axis_index("track")
    core = lax.rem(track, 2)
    finish, after = stream(adj_ref, slots, sems, lambda b: (slice(None), rows_of(b, BLOCK)))

    def put(tile, x):
        high, low = split_hi_lo(x.T)
        at = rows_of(tile, TILE)
        phi[:, at] = high
        plo[:, at] = low

    for d in range(8):
        z = lax.rem(lax.div(track, 2) + d, 8)
        put(2 * z + core, blocks[d][...])
        put(2 * z + 1 - core, theirs_ref[d])

    def one(b, carry):
        at = rows_of(b, BLOCK)
        hi, lo = finish(b)
        out = jnp.dot(phi[...], hi, preferred_element_type=F32)
        out += jnp.dot(plo[...], hi, preferred_element_type=F32)
        out += jnp.dot(phi[...], lo, preferred_element_type=F32)
        out_ref[at, :] = out.T
        after(b)
        return carry

    lax.fori_loop(0, BLOCKS, one, 0)


def track_sums(blocks, theirs, adj):
    return pl.pallas_call(
        track_kernel,
        in_specs=[VMEM] * 9 + [HBM],
        out_specs=VMEM,
        scratch_shapes=[pltpu.VMEM((2 * EMB, SIZE), BF16)] * 2
        + [pltpu.VMEM((DEPTH, 2, SIZE, BLOCK), BF16)]
        + STREAM,
        out_shape=jax.ShapeDtypeStruct((SIZE, 2 * EMB), F32),
        compiler_params=pltpu.CompilerParams(vmem_limit_bytes=46 * MIB),
        cost_estimate=cost(MIB),
    )(*blocks, theirs, adj)


def user_kernel(panel_ref, adj_ref, keep_ref, send_ref, phi, plo, sums, slots, sems):
    track = lax.axis_index("track")
    core = lax.rem(track, 2)

    def block(b):
        return rows_of(lax.rem(lax.div(track, 2) + b, 8), BLOCK)

    finish, after = stream(adj_ref, slots, sems, lambda b: (block(b), slice(None)))

    def tile(c, carry):
        for u in range(0, TILES, 2):
            pair = jnp.concatenate([panel_ref[u, c], panel_ref[u + 1, c]], axis=0)
            high, low = split_hi_lo(pair)
            at = rows_of(c * (TILES // 2) + u // 2, 16)
            phi[at, :] = high
            plo[at, :] = low
        return carry

    lax.fori_loop(0, TILES, tile, 0)

    def one(b, carry):
        hi, lo = finish(b)
        out = jnp.dot(hi, phi[...], preferred_element_type=F32)
        out += jnp.dot(lo, phi[...], preferred_element_type=F32)
        out += jnp.dot(hi, plo[...], preferred_element_type=F32)
        sums[...] = out
        after(b)
        keep_ref[b] = sums[rows_of(core, TILE), :]
        send_ref[b] = sums[rows_of(1 - core, TILE), :]
        return carry

    lax.fori_loop(0, BLOCKS, one, 0)


def user_sums(panel, adj):
    return pl.pallas_call(
        user_kernel,
        in_specs=[VMEM, HBM],
        out_specs=[VMEM] * 2,
        scratch_shapes=[
            pltpu.VMEM((SIZE, 2 * EMB), BF16),
            pltpu.VMEM((SIZE, 2 * EMB), BF16),
            pltpu.VMEM((BLOCK, 2 * EMB), F32),
            pltpu.VMEM((DEPTH, 2, BLOCK, SIZE), BF16),
        ]
        + STREAM,
        out_shape=[jax.ShapeDtypeStruct((8, TILE, 2 * EMB), F32)] * 2,
        compiler_params=pltpu.CompilerParams(vmem_limit_bytes=46 * MIB),
        cost_estimate=cost(MIB),
    )(panel, adj)


def pack_kernel(*refs):
    for d in range(8):
        refs[8][d] = refs[d][...]


def pack(blocks):
    return pl.pallas_call(
        pack_kernel,
        in_specs=[VMEM] * 8,
        out_specs=VMEM,
        out_shape=jax.ShapeDtypeStruct((8, TILE, 2 * EMB), F32),
        compiler_params=pltpu.CompilerParams(vmem_limit_bytes=4 * MIB),
        cost_estimate=cost(2 * MIB),
    )(*blocks)


def shift_z(x, by):
    pairs = [(2 * z + c, 2 * ((z + by) % 8) + c) for z in range(8) for c in range(2)]
    return lax.ppermute(x, "track", pairs)


def swap_core(x):
    return lax.ppermute(x, "track", [(t, t ^ 1) for t in range(16)])


def body(
    user_emb,
    user_cot,
    track_emb,
    track_cot,
    user_degree,
    track_degree,
    tile_vals,
    tile_rows,
    tile_cols,
    tile_count,
):
    user = lax.axis_index("user").astype(jnp.int32)
    user_scale = 1.0 / jnp.sqrt(user_degree.astype(F32))
    track_scale = 1.0 / jnp.sqrt(track_degree.astype(F32))

    rows = TILE // TILES
    scales = track_scale.reshape(TILES, TILE, 1)

    def part(x):
        x = x.reshape(TILES, TILE, EMB) * scales
        return lax.dynamic_slice_in_dim(x, user * rows, rows, 1)

    moving = jnp.concatenate(
        [part(track_emb), part(track_cot), scales.reshape(TILES, 1, TILE)], axis=1
    )
    moving, user_emb, user_cot = lax.optimization_barrier((moving, user_emb, user_cot))
    user_piece = jnp.concatenate([user_emb, user_cot], axis=1) * user_scale[:, None]
    arrived = lax.all_to_all(moving, "track", split_axis=0, concat_axis=0, tiled=True)
    blocks = [user_piece] + [None] * 7
    for d in range(1, 4):
        blocks[d] = shift_z(blocks[d - 1], -1)
        blocks[8 - d] = shift_z(blocks[(9 - d) % 8], 1)
        if d == 2:
            tiles = (
                tile_vals.reshape(SLOTS, TILE, TILE),
                tile_rows.reshape(SLOTS),
                tile_cols.reshape(SLOTS),
                tile_count.reshape(1),
            )
            adj = build(0, *tiles)
            arrived, blocks[2], blocks[6], adj = lax.optimization_barrier(
                (arrived, blocks[2], blocks[6], adj)
            )
    blocks[4] = shift_z(blocks[3], -1)
    adj = build(1, *tiles, adj)

    scale_rows = arrived[:, 2 * rows]
    share = jnp.concatenate([arrived[:, :rows], arrived[:, rows : 2 * rows]], axis=2)
    panel = lax.all_to_all(
        jnp.broadcast_to(share, (TILES,) + share.shape), "user", split_axis=0, concat_axis=0
    )
    theirs = swap_core(pack(blocks))
    to_tracks = track_sums(blocks, theirs, adj)
    to_tracks, panel = lax.optimization_barrier((to_tracks, panel))
    keep, send = user_sums(panel, adj)
    own_scale = lax.dynamic_slice_in_dim(scale_rows, user, 1, 0).reshape(TILE, 1)
    landed = lax.all_to_all(
        to_tracks.reshape(TILES, TILE, 2 * EMB), "user", split_axis=0, concat_axis=0, tiled=True
    )
    got = swap_core(send)
    up, down = lax.optimization_barrier((keep[4] + got[4], keep[5] + got[5]))
    for d in (3, 2, 1):
        up, down = shift_z(up, 1), shift_z(down, -1)
        if d == 2:
            up, down, landed = lax.optimization_barrier((up, down, landed))
        up = up + (keep[d] + got[d])
        if d > 1:
            down = down + (keep[9 - d] + got[9 - d])
        up, down = lax.optimization_barrier((up, down))
    up = shift_z(up, 1)
    user_total = (keep[0] + got[0] + up + down) * user_scale[:, None]
    track_total = (jnp.sum(landed, axis=0) * own_scale).reshape(1, 1, TILE, 2 * EMB)
    return (
        user_total[:, :EMB],
        user_total[:, EMB:],
        track_total[..., :EMB],
        track_total[..., EMB:],
    )


def solution(mesh):
    placed = (
        P(("user", "track"), None),
        P(("user", "track"), None),
        P("track", None),
        P("track", None),
        P(("user", "track")),
        P("track"),
        P("user", "track", None, None, None),
        P("user", "track", None),
        P("user", "track", None),
        P("user", "track"),
    )
    return jax.shard_map(
        body,
        mesh=mesh,
        in_specs=placed,
        out_specs=(
            P(("user", "track"), None),
            P(("user", "track"), None),
            P("user", "track", None, None),
            P("user", "track", None, None),
        ),
        check_vma=False,
    )
```

```python
import functools

import jax
import jax.numpy as jnp
from jax import lax
from jax.experimental import pallas as pl
from jax.experimental.pallas import tpu as pltpu
from jax.sharding import PartitionSpec as P

TILE = 128
TILES = 16
EMB = 128
SLOTS = 128
SLOT_STEP = 16
HALF = TILES // 2
BLOCK = 256
MIB = 1 << 20
LATE = (True, 2)
F32 = jnp.float32
BF16 = jnp.bfloat16


def rows_of(i, size):
    return pl.ds(pl.multiple_of(i * size, size), size)


def split_hi_lo(x):
    hi = x.astype(BF16)
    return hi, (x - hi.astype(F32)).astype(BF16)


def build_kernel(half, row_ref, col_ref, count_ref, vals_ref, *refs):
    out_ref, slots, dense, hi, lo, sems = refs[-6:]
    loads = SLOTS // SLOT_STEP
    copies = []
    for i in range(loads):
        part = pl.ds(i * SLOT_STEP, SLOT_STEP)
        copies.append(pltpu.make_async_copy(vals_ref.at[part], slots.at[part], sems.at[i]))
        copies[-1].start()

    def clear(i, carry):
        dense[i] = jnp.zeros((TILE, TILE), F32)
        return carry

    lax.fori_loop(0, HALF * TILES, clear, 0)

    def add(s, carry):
        row = row_ref[s] - half * HALF

        @pl.when((row >= 0) & (row < HALF))
        def _():
            dense[row * TILES + col_ref[s]] += slots[s]

        return carry

    for i in range(loads):
        copies[i].wait()
        live = jnp.clip(count_ref[0], i * SLOT_STEP, (i + 1) * SLOT_STEP)
        lax.fori_loop(i * SLOT_STEP, live, add, 0)

    copies = []
    for b in range(HALF // 2):

        def pack(r, carry):
            rows = rows_of(r, TILE)
            for c in range(TILES):
                high, low = split_hi_lo(dense[r * TILES + c])
                hi[rows, c * TILE : (c + 1) * TILE] = high
                lo[rows, c * TILE : (c + 1) * TILE] = low
            return carry

        lax.fori_loop(2 * b, 2 * b + 2, pack, 0)
        rows = pl.ds(b * BLOCK, BLOCK)
        there = pl.ds(half * HALF * TILE + b * BLOCK, BLOCK)
        copies.append(pltpu.make_async_copy(hi.at[rows], out_ref.at[0, there], sems.at[2 * b]))
        copies.append(pltpu.make_async_copy(lo.at[rows], out_ref.at[1, there], sems.at[2 * b + 1]))
        copies[-2].start()
        copies[-1].start()
    for copy in copies:
        copy.wait()


VMEM = pl.BlockSpec(memory_space=pltpu.VMEM)
SMEM = pl.BlockSpec(memory_space=pltpu.SMEM)
HBM = pl.BlockSpec(memory_space=pltpu.HBM)
SIZE = TILES * TILE
BLOCKS = SIZE // BLOCK
DEPTH = 3
STREAM = [pltpu.SemaphoreType.DMA((DEPTH, 2))]


def cost(nbytes):
    return pl.CostEstimate(flops=0, bytes_accessed=nbytes, transcendentals=0)


def build(half, vals, rows, cols, count, *others):
    return pl.pallas_call(
        functools.partial(build_kernel, half),
        in_specs=[SMEM, SMEM, SMEM, HBM] + [HBM] * len(others),
        out_specs=HBM,
        out_shape=jax.ShapeDtypeStruct((2, SIZE, SIZE), BF16),
        input_output_aliases={4: 0} if others else {},
        scratch_shapes=[
            pltpu.VMEM((SLOTS, TILE, TILE), F32),
            pltpu.VMEM((HALF * TILES, TILE, TILE), F32),
            pltpu.VMEM((HALF * TILE, SIZE), BF16),
            pltpu.VMEM((HALF * TILE, SIZE), BF16),
            pltpu.SemaphoreType.DMA((SLOTS // SLOT_STEP,)),
        ],
        compiler_params=pltpu.CompilerParams(vmem_limit_bytes=46 * MIB),
        cost_estimate=cost(12 * MIB * half),
    )(rows, cols, count, vals, *others)


def stream(adj_ref, slots, sems, part):
    def copies(b):
        at = part(b)
        slot = lax.rem(b, DEPTH)
        return [
            pltpu.make_async_copy(adj_ref.at[(k,) + at], slots.at[slot, k], sems.at[slot, k])
            for k in range(2)
        ]

    def begin(b):
        for copy in copies(b):
            copy.start()

    def finish(b):
        for copy in copies(b):
            copy.wait()
        slot = lax.rem(b, DEPTH)
        return slots[slot, 0], slots[slot, 1]

    def after(b):
        @pl.when(b + DEPTH < BLOCKS)
        def _():
            begin(b + DEPTH)

    for b in range(DEPTH):
        begin(b)
    return finish, after


def track_kernel(mine_ref, theirs_ref, adj_ref, out_ref, phi, plo, slots, sems):
    track = lax.axis_index("track")
    core = lax.rem(track, 2)
    finish, after = stream(adj_ref, slots, sems, lambda b: (slice(None), rows_of(b, BLOCK)))

    def put(tile, x):
        high, low = split_hi_lo(x.T)
        at = rows_of(tile, TILE)
        phi[:, at] = high
        plo[:, at] = low

    def both(d, carry):
        z = lax.rem(lax.div(track, 2) + d, 8)
        put(2 * z + core, mine_ref[d])
        put(2 * z + 1 - core, theirs_ref[d])
        return carry

    lax.fori_loop(0, 8, both, 0)

    def one(b, carry):
        at = rows_of(b, BLOCK)
        hi, lo = finish(b)
        out = jnp.dot(phi[...], hi, preferred_element_type=F32)
        out += jnp.dot(plo[...], hi, preferred_element_type=F32)
        out += jnp.dot(phi[...], lo, preferred_element_type=F32)
        out_ref[at, :] = out.T
        after(b)
        return carry

    lax.fori_loop(0, BLOCKS, one, 0)


def track_sums(mine, theirs, adj):
    return pl.pallas_call(
        track_kernel,
        in_specs=[VMEM, VMEM, HBM],
        out_specs=VMEM,
        scratch_shapes=[pltpu.VMEM((2 * EMB, SIZE), BF16)] * 2
        + [pltpu.VMEM((DEPTH, 2, SIZE, BLOCK), BF16)]
        + STREAM,
        out_shape=jax.ShapeDtypeStruct((SIZE, 2 * EMB), F32),
        compiler_params=pltpu.CompilerParams(vmem_limit_bytes=46 * MIB),
        cost_estimate=cost(MIB),
    )(mine, theirs, adj)


def user_kernel(panel_ref, adj_ref, keep_a, keep_b, send_a, send_b, phi, plo, sums, slots, sems):
    track = lax.axis_index("track")
    core = lax.rem(track, 2)

    def block(b):
        step = lax.div(b, 2)
        ahead = jnp.where(lax.rem(b, 2) == 0, 4 - step, 5 + step)
        return rows_of(lax.rem(lax.div(track, 2) + ahead, 8), BLOCK)

    finish, after = stream(adj_ref, slots, sems, lambda b: (block(b), slice(None)))

    def tile(c, carry):
        for u in range(0, TILES, 2):
            pair = jnp.concatenate([panel_ref[u, c], panel_ref[u + 1, c]], axis=0)
            high, low = split_hi_lo(pair)
            at = rows_of(c * (TILES // 2) + u // 2, 16)
            phi[at, :] = high
            plo[at, :] = low
        return carry

    lax.fori_loop(0, TILES, tile, 0)

    def one(b, carry):
        hi, lo = finish(b)
        out = jnp.dot(hi, phi[...], preferred_element_type=F32)
        out += jnp.dot(lo, phi[...], preferred_element_type=F32)
        out += jnp.dot(hi, plo[...], preferred_element_type=F32)
        sums[...] = out
        after(b)

        @pl.when(b < 4)
        def _():
            keep_a[b] = sums[rows_of(core, TILE), :]
            send_a[b] = sums[rows_of(1 - core, TILE), :]

        @pl.when(b >= 4)
        def _():
            keep_b[b - 4] = sums[rows_of(core, TILE), :]
            send_b[b - 4] = sums[rows_of(1 - core, TILE), :]

        return carry

    lax.fori_loop(0, BLOCKS, one, 0)


def user_sums(panel, adj):
    return pl.pallas_call(
        user_kernel,
        in_specs=[VMEM, HBM],
        out_specs=[VMEM] * 4,
        scratch_shapes=[
            pltpu.VMEM((SIZE, 2 * EMB), BF16),
            pltpu.VMEM((SIZE, 2 * EMB), BF16),
            pltpu.VMEM((BLOCK, 2 * EMB), F32),
            pltpu.VMEM((DEPTH, 2, BLOCK, SIZE), BF16),
        ]
        + STREAM,
        out_shape=[jax.ShapeDtypeStruct((4, TILE, 2 * EMB), F32)] * 4,
        compiler_params=pltpu.CompilerParams(vmem_limit_bytes=46 * MIB),
        cost_estimate=cost(MIB),
    )(panel, adj)


def pack_kernel(*refs):
    for d in range(8):
        refs[8][d] = refs[d][...]


def pack(blocks):
    return pl.pallas_call(
        pack_kernel,
        in_specs=[VMEM] * 8,
        out_specs=VMEM,
        out_shape=jax.ShapeDtypeStruct((8, TILE, 2 * EMB), F32),
        compiler_params=pltpu.CompilerParams(vmem_limit_bytes=4 * MIB),
        cost_estimate=cost(2 * MIB),
    )(*blocks)


def shift_z(x, by):
    pairs = [(2 * z + c, 2 * ((z + by) % 8) + c) for z in range(8) for c in range(2)]
    return lax.ppermute(x, "track", pairs)


def swap_core(x):
    return lax.ppermute(x, "track", [(t, t ^ 1) for t in range(16)])


def body(
    user_emb,
    user_cot,
    track_emb,
    track_cot,
    user_degree,
    track_degree,
    tile_vals,
    tile_rows,
    tile_cols,
    tile_count,
):
    user = lax.axis_index("user").astype(jnp.int32)
    user_scale = 1.0 / jnp.sqrt(user_degree.astype(F32))
    track_scale = 1.0 / jnp.sqrt(track_degree.astype(F32))

    rows = TILE // TILES
    scales = track_scale.reshape(TILES, TILE, 1)

    def part(x):
        x = x.reshape(TILES, TILE, EMB) * scales
        return lax.dynamic_slice_in_dim(x, user * rows, rows, 1)

    moving = jnp.concatenate(
        [part(track_emb), part(track_cot), scales.reshape(TILES, 1, TILE)], axis=1
    )
    moving, user_emb, user_cot = lax.optimization_barrier((moving, user_emb, user_cot))
    user_piece = jnp.concatenate([user_emb, user_cot], axis=1) * user_scale[:, None]
    arrived = lax.all_to_all(moving, "track", split_axis=0, concat_axis=0, tiled=True)
    blocks = [user_piece] + [None] * 7
    for d in range(1, 4):
        blocks[d] = shift_z(blocks[d - 1], -1)
        blocks[8 - d] = shift_z(blocks[(9 - d) % 8], 1)
        if d == 2:
            tiles = (
                tile_vals.reshape(SLOTS, TILE, TILE),
                tile_rows.reshape(SLOTS),
                tile_cols.reshape(SLOTS),
                tile_count.reshape(1),
            )
            adj = build(0, *tiles)
            arrived, blocks[2], blocks[6], adj = lax.optimization_barrier(
                (arrived, blocks[2], blocks[6], adj)
            )
    blocks[4] = shift_z(blocks[3], -1)
    adj = build(1, *tiles, adj)

    scale_rows = arrived[:, 2 * rows]
    share = jnp.concatenate([arrived[:, :rows], arrived[:, rows : 2 * rows]], axis=2)
    panel = lax.all_to_all(
        jnp.broadcast_to(share, (TILES,) + share.shape), "user", split_axis=0, concat_axis=0
    )
    mine = pack(blocks)
    theirs = swap_core(mine)
    to_tracks = track_sums(mine, theirs, adj)
    to_tracks, panel = lax.optimization_barrier((to_tracks, panel))
    keep_a, keep_b, send_a, send_b = user_sums(panel, adj)
    own_scale = lax.dynamic_slice_in_dim(scale_rows, user, 1, 0).reshape(TILE, 1)
    landed = lax.all_to_all(
        to_tracks.reshape(TILES, TILE, 2 * EMB), "user", split_axis=0, concat_axis=0, tiled=True
    )
    got_a, got_b = swap_core(send_a), swap_core(send_b)
    up, down = lax.optimization_barrier((keep_a[0] + got_a[0], keep_a[1] + got_a[1]))
    for keep, got, d in ((keep_a, got_a, 2), (keep_b, got_b, 0), (keep_b, got_b, 2)):
        up, down = shift_z(up, 1), shift_z(down, -1)
        if LATE == (keep is keep_b, d):
            up, down, landed = lax.optimization_barrier((up, down, landed))
        up = up + (keep[d] + got[d])
        if keep is keep_a or d == 0:
            down = down + (keep[d + 1] + got[d + 1])
        up, down = lax.optimization_barrier((up, down))
    up = shift_z(up, 1)
    user_total = (keep_b[3] + got_b[3] + up + down) * user_scale[:, None]
    track_total = (jnp.sum(landed, axis=0) * own_scale).reshape(1, 1, TILE, 2 * EMB)
    return (
        user_total[:, :EMB],
        user_total[:, EMB:],
        track_total[..., :EMB],
        track_total[..., EMB:],
    )


def solution(mesh):
    placed = (
        P(("user", "track"), None),
        P(("user", "track"), None),
        P("track", None),
        P("track", None),
        P(("user", "track")),
        P("track"),
        P("user", "track", None, None, None),
        P("user", "track", None),
        P("user", "track", None),
        P("user", "track"),
    )
    return jax.shard_map(
        body,
        mesh=mesh,
        in_specs=placed,
        out_specs=(
            P(("user", "track"), None),
            P(("user", "track"), None),
            P("user", "track", None, None),
            P("user", "track", None, None),
        ),
        check_vma=False,
    )
```

```python
import functools

import jax
import jax.numpy as jnp
from jax import lax
from jax.experimental import pallas as pl
from jax.experimental.pallas import tpu as pltpu
from jax.sharding import PartitionSpec as P

TILE = 128
TILES = 16
EMB = 128
SLOTS = 128
HALF = TILES // 2
BLOCK = 256
MIB = 1 << 20
LATE = (True, 2)
F32 = jnp.float32
BF16 = jnp.bfloat16


def rows_of(i, size):
    return pl.ds(pl.multiple_of(i * size, size), size)


def split_hi_lo(x):
    hi = x.astype(BF16)
    return hi, (x - hi.astype(F32)).astype(BF16)


def build_kernel(half, row_ref, col_ref, count_ref, vals_ref, *refs):
    out_ref, slots, dense, hi, lo, sems = refs[-6:]

    def load(s):
        return pltpu.make_async_copy(vals_ref.at[s], slots.at[s], sems.at[s])

    def if_mine(s, do):
        row = row_ref[s] - half * HALF
        pl.when((row >= 0) & (row < HALF))(lambda: do(row))

    def fetch(s, carry):
        if_mine(s, lambda row: load(s).start())
        return carry

    def clear(i, carry):
        dense[i] = jnp.zeros((TILE, TILE), F32)
        return carry

    def add(s, carry):
        def do(row):
            load(s).wait()
            dense[row * TILES + col_ref[s]] += slots[s]

        if_mine(s, do)
        return carry

    live = jnp.clip(count_ref[0], 0, SLOTS)
    lax.fori_loop(0, live, fetch, 0)
    lax.fori_loop(0, HALF * TILES, clear, 0)
    lax.fori_loop(0, live, add, 0)

    copies = []
    for b in range(HALF // 2):

        def pack(r, carry):
            rows = rows_of(r, TILE)
            for c in range(TILES):
                high, low = split_hi_lo(dense[r * TILES + c])
                hi[rows, c * TILE : (c + 1) * TILE] = high
                lo[rows, c * TILE : (c + 1) * TILE] = low
            return carry

        lax.fori_loop(2 * b, 2 * b + 2, pack, 0)
        rows = pl.ds(b * BLOCK, BLOCK)
        there = pl.ds(half * HALF * TILE + b * BLOCK, BLOCK)
        copies.append(pltpu.make_async_copy(hi.at[rows], out_ref.at[0, there], sems.at[2 * b]))
        copies.append(pltpu.make_async_copy(lo.at[rows], out_ref.at[1, there], sems.at[2 * b + 1]))
        copies[-2].start()
        copies[-1].start()
    for copy in copies:
        copy.wait()


VMEM = pl.BlockSpec(memory_space=pltpu.VMEM)
SMEM = pl.BlockSpec(memory_space=pltpu.SMEM)
HBM = pl.BlockSpec(memory_space=pltpu.HBM)
SIZE = TILES * TILE
BLOCKS = SIZE // BLOCK
DEPTH = 3
STREAM = [pltpu.SemaphoreType.DMA((DEPTH, 2))]


def cost(nbytes):
    return pl.CostEstimate(flops=0, bytes_accessed=nbytes, transcendentals=0)


def build(half, vals, rows, cols, count, *others):
    return pl.pallas_call(
        functools.partial(build_kernel, half),
        in_specs=[SMEM, SMEM, SMEM, HBM] + [HBM] * len(others),
        out_specs=HBM,
        out_shape=jax.ShapeDtypeStruct((2, SIZE, SIZE), BF16),
        input_output_aliases={4: 0} if others else {},
        scratch_shapes=[
            pltpu.VMEM((SLOTS, TILE, TILE), F32),
            pltpu.VMEM((HALF * TILES, TILE, TILE), F32),
            pltpu.VMEM((HALF * TILE, SIZE), BF16),
            pltpu.VMEM((HALF * TILE, SIZE), BF16),
            pltpu.SemaphoreType.DMA((SLOTS,)),
        ],
        compiler_params=pltpu.CompilerParams(vmem_limit_bytes=46 * MIB),
        cost_estimate=cost(12 * MIB * half),
    )(rows, cols, count, vals, *others)


def stream(adj_ref, slots, sems, part):
    def copies(b):
        at = part(b)
        slot = lax.rem(b, DEPTH)
        return [
            pltpu.make_async_copy(adj_ref.at[(k,) + at], slots.at[slot, k], sems.at[slot, k])
            for k in range(2)
        ]

    def begin(b):
        for copy in copies(b):
            copy.start()

    def finish(b):
        for copy in copies(b):
            copy.wait()
        slot = lax.rem(b, DEPTH)
        return slots[slot, 0], slots[slot, 1]

    def after(b):
        @pl.when(b + DEPTH < BLOCKS)
        def _():
            begin(b + DEPTH)

    for b in range(DEPTH):
        begin(b)
    return finish, after


def track_kernel(mine_ref, theirs_ref, adj_ref, out_ref, phi, plo, slots, sems):
    track = lax.axis_index("track")
    core = lax.rem(track, 2)
    finish, after = stream(adj_ref, slots, sems, lambda b: (slice(None), rows_of(b, BLOCK)))

    def put(tile, x):
        high, low = split_hi_lo(x.T)
        at = rows_of(tile, TILE)
        phi[:, at] = high
        plo[:, at] = low

    def both(d, carry):
        z = lax.rem(lax.div(track, 2) + d, 8)
        put(2 * z + core, mine_ref[d])
        put(2 * z + 1 - core, theirs_ref[d])
        return carry

    lax.fori_loop(0, 8, both, 0)

    def one(b, carry):
        at = rows_of(b, BLOCK)
        hi, lo = finish(b)
        out = jnp.dot(phi[...], hi, preferred_element_type=F32)
        out += jnp.dot(plo[...], hi, preferred_element_type=F32)
        out += jnp.dot(phi[...], lo, preferred_element_type=F32)
        out_ref[at, :] = out.T
        after(b)
        return carry

    lax.fori_loop(0, BLOCKS, one, 0)


def track_sums(mine, theirs, adj):
    return pl.pallas_call(
        track_kernel,
        in_specs=[VMEM, VMEM, HBM],
        out_specs=VMEM,
        scratch_shapes=[pltpu.VMEM((2 * EMB, SIZE), BF16)] * 2
        + [pltpu.VMEM((DEPTH, 2, SIZE, BLOCK), BF16)]
        + STREAM,
        out_shape=jax.ShapeDtypeStruct((SIZE, 2 * EMB), F32),
        compiler_params=pltpu.CompilerParams(vmem_limit_bytes=46 * MIB),
        cost_estimate=cost(MIB),
    )(mine, theirs, adj)


def user_kernel(panel_ref, adj_ref, keep_a, keep_b, send_a, send_b, phi, plo, sums, slots, sems):
    track = lax.axis_index("track")
    core = lax.rem(track, 2)

    def block(b):
        step = lax.div(b, 2)
        ahead = jnp.where(lax.rem(b, 2) == 0, 4 - step, 5 + step)
        return rows_of(lax.rem(lax.div(track, 2) + ahead, 8), BLOCK)

    finish, after = stream(adj_ref, slots, sems, lambda b: (block(b), slice(None)))

    def tile(c, carry):
        for u in range(0, TILES, 2):
            pair = jnp.concatenate([panel_ref[u, c], panel_ref[u + 1, c]], axis=0)
            high, low = split_hi_lo(pair)
            at = rows_of(c * (TILES // 2) + u // 2, 16)
            phi[at, :] = high
            plo[at, :] = low
        return carry

    lax.fori_loop(0, TILES, tile, 0)

    def one(b, carry):
        hi, lo = finish(b)
        out = jnp.dot(hi, phi[...], preferred_element_type=F32)
        out += jnp.dot(lo, phi[...], preferred_element_type=F32)
        out += jnp.dot(hi, plo[...], preferred_element_type=F32)
        sums[...] = out
        after(b)

        @pl.when(b < 4)
        def _():
            keep_a[b] = sums[rows_of(core, TILE), :]
            send_a[b] = sums[rows_of(1 - core, TILE), :]

        @pl.when(b >= 4)
        def _():
            keep_b[b - 4] = sums[rows_of(core, TILE), :]
            send_b[b - 4] = sums[rows_of(1 - core, TILE), :]

        return carry

    lax.fori_loop(0, BLOCKS, one, 0)


def user_sums(panel, adj):
    return pl.pallas_call(
        user_kernel,
        in_specs=[VMEM, HBM],
        out_specs=[VMEM] * 4,
        scratch_shapes=[
            pltpu.VMEM((SIZE, 2 * EMB), BF16),
            pltpu.VMEM((SIZE, 2 * EMB), BF16),
            pltpu.VMEM((BLOCK, 2 * EMB), F32),
            pltpu.VMEM((DEPTH, 2, BLOCK, SIZE), BF16),
        ]
        + STREAM,
        out_shape=[jax.ShapeDtypeStruct((4, TILE, 2 * EMB), F32)] * 4,
        compiler_params=pltpu.CompilerParams(vmem_limit_bytes=46 * MIB),
        cost_estimate=cost(MIB),
    )(panel, adj)


def pack_kernel(*refs):
    for d in range(8):
        refs[8][d] = refs[d][...]


def pack(blocks):
    return pl.pallas_call(
        pack_kernel,
        in_specs=[VMEM] * 8,
        out_specs=VMEM,
        out_shape=jax.ShapeDtypeStruct((8, TILE, 2 * EMB), F32),
        compiler_params=pltpu.CompilerParams(vmem_limit_bytes=4 * MIB),
        cost_estimate=cost(2 * MIB),
    )(*blocks)


def shift_z(x, by):
    pairs = [(2 * z + c, 2 * ((z + by) % 8) + c) for z in range(8) for c in range(2)]
    return lax.ppermute(x, "track", pairs)


def swap_core(x):
    return lax.ppermute(x, "track", [(t, t ^ 1) for t in range(16)])


def body(
    user_emb,
    user_cot,
    track_emb,
    track_cot,
    user_degree,
    track_degree,
    tile_vals,
    tile_rows,
    tile_cols,
    tile_count,
):
    user = lax.axis_index("user").astype(jnp.int32)
    user_scale = 1.0 / jnp.sqrt(user_degree.astype(F32))
    track_scale = 1.0 / jnp.sqrt(track_degree.astype(F32))

    rows = TILE // TILES
    scales = track_scale.reshape(TILES, TILE, 1)

    def part(x):
        x = x.reshape(TILES, TILE, EMB) * scales
        return lax.dynamic_slice_in_dim(x, user * rows, rows, 1)

    moving = jnp.concatenate(
        [part(track_emb), part(track_cot), scales.reshape(TILES, 1, TILE)], axis=1
    )
    moving, user_emb, user_cot = lax.optimization_barrier((moving, user_emb, user_cot))
    user_piece = jnp.concatenate([user_emb, user_cot], axis=1) * user_scale[:, None]
    arrived = lax.all_to_all(moving, "track", split_axis=0, concat_axis=0, tiled=True)
    blocks = [user_piece] + [None] * 7
    for d in range(1, 4):
        blocks[d] = shift_z(blocks[d - 1], -1)
        blocks[8 - d] = shift_z(blocks[(9 - d) % 8], 1)
        if d == 2:
            tiles = (
                tile_vals.reshape(SLOTS, TILE, TILE),
                tile_rows.reshape(SLOTS),
                tile_cols.reshape(SLOTS),
                tile_count.reshape(1),
            )
            adj = build(0, *tiles)
            arrived, blocks[2], blocks[6], adj = lax.optimization_barrier(
                (arrived, blocks[2], blocks[6], adj)
            )
    blocks[4] = shift_z(blocks[3], -1)
    adj = build(1, *tiles, adj)

    scale_rows = arrived[:, 2 * rows]
    share = jnp.concatenate([arrived[:, :rows], arrived[:, rows : 2 * rows]], axis=2)
    panel = lax.all_to_all(
        jnp.broadcast_to(share, (TILES,) + share.shape), "user", split_axis=0, concat_axis=0
    )
    mine = pack(blocks)
    theirs = swap_core(mine)
    to_tracks = track_sums(mine, theirs, adj)
    to_tracks, panel = lax.optimization_barrier((to_tracks, panel))
    keep_a, keep_b, send_a, send_b = user_sums(panel, adj)
    own_scale = lax.dynamic_slice_in_dim(scale_rows, user, 1, 0).reshape(TILE, 1)
    landed = lax.all_to_all(
        to_tracks.reshape(TILES, TILE, 2 * EMB), "user", split_axis=0, concat_axis=0, tiled=True
    )
    got_a, got_b = swap_core(send_a), swap_core(send_b)
    up, down = lax.optimization_barrier((keep_a[0] + got_a[0], keep_a[1] + got_a[1]))
    for keep, got, d in ((keep_a, got_a, 2), (keep_b, got_b, 0), (keep_b, got_b, 2)):
        up, down = shift_z(up, 1), shift_z(down, -1)
        if LATE == (keep is keep_b, d):
            up, down, landed = lax.optimization_barrier((up, down, landed))
        up = up + (keep[d] + got[d])
        if keep is keep_a or d == 0:
            down = down + (keep[d + 1] + got[d + 1])
        up, down = lax.optimization_barrier((up, down))
    up = shift_z(up, 1)
    user_total = (keep_b[3] + got_b[3] + up + down) * user_scale[:, None]
    track_total = (jnp.sum(landed, axis=0) * own_scale).reshape(1, 1, TILE, 2 * EMB)
    return (
        user_total[:, :EMB],
        user_total[:, EMB:],
        track_total[..., :EMB],
        track_total[..., EMB:],
    )


def solution(mesh):
    placed = (
        P(("user", "track"), None),
        P(("user", "track"), None),
        P("track", None),
        P("track", None),
        P(("user", "track")),
        P("track"),
        P("user", "track", None, None, None),
        P("user", "track", None),
        P("user", "track", None),
        P("user", "track"),
    )
    return jax.shard_map(
        body,
        mesh=mesh,
        in_specs=placed,
        out_specs=(
            P(("user", "track"), None),
            P(("user", "track"), None),
            P("user", "track", None, None),
            P("user", "track", None, None),
        ),
        check_vma=False,
    )
```
